32 devices in a mesh: depth: 8 (over z, y), freq: 4 (over x, core).
Axes of the slice: x: 2, y: 2, z: 4, core: 2. Of those that a mesh axis runs over, the one named last changes fastest.
Arguments:
- extrap: bfloat16 [8, 4, 2, 1024, 1024], P('depth', 'freq'), may hold values from -0.125 to 0.125
- source_field: bfloat16 [4, 128, 2, 1024], P('freq'), may hold values from -6 to 6
- record_field: bfloat16 [4, 128, 2, 1024], P('freq'), may hold values from -6 to 6
- shot_of_record: int32 [128], replicated, may hold values from 0 to 127, each once
- freq_index: int32 [4], P('freq'), may hold values from 0 to 31, as said below
- angle_lag: int32 [1024, 256], replicated, may hold values from 0 to 7
Outputs:
- gathers: float32 [1024, 8, 256], P(('freq', 'depth'))
The draws below stay inside these ranges and needn't reach their ends.
Inputs may be any that keep to these rules, and one draw needn't show every extreme that they name: `shot_of_record`: each shot is named once. `freq_index`: the frequency numbers are distinct, and the largest one, 31, is always held by some slot.
All inputs are finite; a program needn't handle non-finite values.
Results may differ from the reference program's by a relative error of at most 0.035.
Values may be sent and summed in bfloat16 or wider, within the bound.
No kernel may reach another device: no remote copies, remote signals or barrier semaphores. Data moves between devices by JAX's collectives and lax.ppermute only.
A program may use at most 64 MiB of HBM per device.

```python
import math
import jax
import jax.numpy as jnp
from jax import lax

X = 1024
ANGLES = 256
SHOTS = 128
NZ = 8
FREQS = 4


def draw_freq_index(key, part):
    others = jax.random.permutation(jax.random.fold_in(key, 11), 8 * FREQS - 1)[:FREQS - 1]
    values = jnp.concatenate([others.astype(jnp.int32), jnp.full((1,), 8 * FREQS - 1, jnp.int32)])
    order = jax.random.permutation(jax.random.fold_in(key, 12), FREQS)
    return values[order].astype(jnp.int32)


def touch_ends(drawn, rng, smallest, top_value):
    spot = [jax.random.randint(jax.random.fold_in(rng, axis), (), 0, length) for axis, length in enumerate(drawn.shape)]
    widest = drawn.shape.index(max(drawn.shape))
    beside = spot[:widest] + [(spot[widest] + 1) % drawn.shape[widest]] + spot[widest + 1:]
    return drawn.at[tuple(spot)].set(smallest).at[tuple(beside)].set(top_value)


def levels(rng, shape, split, smallest, high):
    def one(dim, blocks):
        heights = jax.random.uniform(jax.random.fold_in(jax.random.fold_in(rng, 6), dim), (blocks,), jnp.float32, smallest / len(split), high / len(split))
        return jnp.repeat(jnp.exp(heights), shape[dim] // blocks).reshape((-1,) + (1,) * (len(shape) - dim - 1))

    loudness = one(*split[0])
    for cut in split[1:]:
        loudness = loudness * one(*cut)
    return loudness


def noise(rng, shape, width, reach, shards=(), held_as=jnp.bfloat16):
    values = width * jax.random.normal(rng, shape, jnp.float32)
    if shards:
        values = values * levels(rng, shape, shards, -0.22, 0.18)
    return jnp.clip(values, -reach, reach).astype(held_as)


def setup_inputs(seed: int = 0) -> dict:
    keys = jax.random.split(jax.random.key(seed), 7)
    extrap = noise(keys[0], (NZ, FREQS, 2, X, X), (2 * X) ** -0.5, 0.125, ((0, 8), (1, 4)))
    source_field = noise(keys[1], (FREQS, SHOTS, 2, X), 1.0, 6.0, ((0, 4),))
    record_field = noise(keys[2], (FREQS, SHOTS, 2, X), 1.0, 6.0, ((0, 4),))
    shot_of_record = jax.random.permutation(keys[3], SHOTS).astype(jnp.int32)
    freq_index = draw_freq_index(jax.random.fold_in(keys[6], 71), 0)
    angle_lag = touch_ends(jax.random.randint(keys[5], (X, ANGLES), 0, NZ), jax.random.fold_in(keys[5], 1), 0, NZ - 1).astype(jnp.int32)
    return dict(extrap=extrap, source_field=source_field, record_field=record_field, shot_of_record=shot_of_record, freq_index=freq_index, angle_lag=angle_lag)


def make_block(real_part, imag_part):
    upper = jnp.concatenate([real_part, imag_part], axis=1)
    lower = jnp.concatenate([-imag_part, real_part], axis=1)
    return jnp.concatenate([upper, lower], axis=0)

def reference(extrap, source_field, record_field, shot_of_record, freq_index, angle_lag):
    points = source_field.shape[3]
    shot_count = source_field.shape[1]
    weights = (freq_index.astype(jnp.float32) + 1.0) / (8 * FREQS)
    factor = 1.0 / math.sqrt(SHOTS * FREQS)
    paired = source_field[:, shot_of_record].reshape(FREQS, shot_count, 2 * points)
    records = jnp.concatenate([record_field[:, :, 1], record_field[:, :, 0]], axis=2)
    source_list = [paired[freq_slot] for freq_slot in range(FREQS)]
    record_list = [records[freq_slot] for freq_slot in range(FREQS)]
    image_list = []
    for depth_level in range(NZ):
        image = jnp.zeros((points, points), jnp.float32)
        for freq_slot in range(FREQS):
            extrapolator = make_block(extrap[depth_level, freq_slot, 0], extrap[depth_level, freq_slot, 1])
            stacked = jnp.concatenate([source_list[freq_slot], record_list[freq_slot]], axis=0)
            advanced = jnp.dot(stacked, extrapolator, preferred_element_type=jnp.float32).astype(jnp.bfloat16)
            source_list[freq_slot] = advanced[:shot_count]
            record_list[freq_slot] = advanced[shot_count:]
            source_stack = advanced[:shot_count].reshape(2 * shot_count, points)
            record_stack = advanced[shot_count:].reshape(shot_count, 2, points)[:, ::-1].reshape(2 * shot_count, points)
            partial_value = lax.dot_general(source_stack, record_stack, (((0,), (0,)), ((), ())), preferred_element_type=jnp.float32)
            image = image + partial_value * (weights[freq_slot] * factor)
        image_list.append(image.astype(jnp.bfloat16))
    images = jnp.stack(image_list, axis=0)
    padded = jnp.concatenate([images, jnp.zeros_like(images)], axis=0)
    stacked_sum = jnp.zeros((points * NZ, ANGLES), jnp.float32)
    for lag_value in range(NZ):
        shifted = jnp.transpose(padded[lag_value:lag_value + NZ], (1, 0, 2)).reshape(points * NZ, points)
        selector = (angle_lag == lag_value).astype(jnp.bfloat16)
        stacked_sum = stacked_sum + jnp.dot(shifted, selector, preferred_element_type=jnp.float32)
    return (stacked_sum / math.sqrt(points)).reshape(points, NZ, ANGLES)
```

```python
import math

import jax
import jax.numpy as jnp
from jax import lax
from jax.sharding import PartitionSpec as P

CHUNKS = 4


def first_round(level):
    return 3 * (level // 2) + level % 2


def pairs_of(round_index, parity, depth_count, chunk_count):
    return [
        (level, level + 1)
        for level in range(parity, depth_count - 1, 2)
        if 0 <= round_index - first_round(level) < chunk_count
    ]


def busy(round_index, parity, depth_count, chunk_count):
    return any(
        0 <= round_index - first_round(level) < chunk_count
        for level in range(parity, depth_count, 2)
    )


def shards(extrap, source_field, record_field, shot_of_record, freq_index, angle_lag):
    level = lax.axis_index("depth")
    depth_count = lax.axis_size("depth")
    freq_count = lax.axis_size("freq")
    freq_slot = lax.axis_index("freq")
    points = source_field.shape[3]
    shot_count = source_field.shape[1]
    chunk_count = CHUNKS
    part = shot_count // chunk_count
    rows = 4 * part
    half_rows = 2 * part

    weights = jnp.concatenate([extrap[0, 0, 0], extrap[0, 0, 1]], axis=1)
    sources = jnp.take(source_field[0], shot_of_record, axis=0)
    records = record_field[0]

    def local_chunk(index):
        span = slice(index * part, (index + 1) * part)
        return jnp.concatenate(
            [sources[span, 0], records[span, 1], sources[span, 1], records[span, 0]], axis=0
        )

    def extend(values):
        product = jnp.dot(values, weights, preferred_element_type=jnp.float32)
        real = product[:half_rows, :points] - product[half_rows:, points:]
        imag = product[:half_rows, points:] + product[half_rows:, :points]
        return jnp.concatenate([real, imag], axis=0).astype(jnp.bfloat16)

    finished = jnp.zeros((chunk_count + 2, rows, points), jnp.bfloat16)
    sent = {}
    round_count = first_round(depth_count - 1) + chunk_count
    my_first = 3 * (level // 2) + level % 2
    for round_index in range(round_count):
        outcome = {}
        for parity in (0, 1):
            if not busy(round_index, parity, depth_count, chunk_count):
                continue
            arrived = sent.get((1 - parity, round_index - 2 + parity))
            entering = arrived
            if parity == 0 and round_index < chunk_count:
                entering = local_chunk(round_index)
                if arrived is not None:
                    entering = jnp.where(level == 0, entering, arrived)
            outcome[parity] = extend(entering)
            pairs = pairs_of(round_index, parity, depth_count, chunk_count)
            if pairs:
                sent[parity, round_index] = lax.ppermute(outcome[parity], "depth", pairs)
        if len(outcome) == 2:
            kept = jnp.where(level % 2 == 0, outcome[0], outcome[1])
        else:
            kept = next(iter(outcome.values()))
        slot = jnp.clip(round_index - my_first, -1, chunk_count) + 1
        finished = lax.dynamic_update_index_in_dim(finished, kept, slot, 0)

    done = finished[1 : chunk_count + 1].reshape(chunk_count, 2, 2, part, points)
    source_stack = done[:, :, 0].reshape(2 * shot_count, points)
    record_stack = done[:, ::-1, 1].reshape(2 * shot_count, points)
    number = freq_index[0].astype(jnp.float32) + 1.0
    scale = 1.0 / (8 * freq_count) / math.sqrt(shot_count * freq_count)

    def correlate(source_part, record_part):
        return lax.dot_general(
            source_part, record_part, (((0,), (0,)), ((), ())), preferred_element_type=jnp.float32
        )

    span = freq_count // 2
    width = points // 2
    upper = (freq_slot // span) % 2 == 1
    partner = [(slot, slot ^ span) for slot in range(freq_count)]
    own_half = jnp.where(upper, source_stack[:, width:], source_stack[:, :width])
    other_half = jnp.where(upper, source_stack[:, :width], source_stack[:, width:])
    payload = jnp.concatenate([record_stack, other_half], axis=1)
    note = jnp.full((16, payload.shape[1]), number, jnp.float32).astype(jnp.bfloat16)
    payload = jnp.concatenate([payload, note], axis=0)
    received = lax.ppermute(payload, "freq", partner)
    their_number = received[2 * shot_count, 0].astype(jnp.float32)
    image = correlate(own_half, record_stack) * (number * scale) + correlate(
        received[: 2 * shot_count, points:], received[: 2 * shot_count, :points]
    ) * (their_number * scale)
    span //= 2
    while span:
        width //= 2
        upper = (freq_slot // span) % 2 == 1
        partner = [(slot, slot ^ span) for slot in range(freq_count)]
        keep = jnp.where(upper, image[width:], image[:width])
        away = jnp.where(upper, image[:width], image[width:]).astype(jnp.bfloat16)
        image = keep + lax.ppermute(away, "freq", partner).astype(jnp.float32)
        span //= 2
    panel = lax.all_to_all(
        image.astype(jnp.bfloat16), "depth", split_axis=0, concat_axis=0, tiled=True
    )
    row_count = panel.shape[0] // depth_count
    angle_count = angle_lag.shape[1]
    lags = jnp.arange(depth_count, dtype=angle_lag.dtype)
    selector = (
        (angle_lag[:, None, :] == lags[None, :, None])
        .astype(jnp.bfloat16)
        .reshape(points, depth_count * angle_count)
    )
    spread = jnp.dot(panel, selector, preferred_element_type=jnp.float32).reshape(
        depth_count, row_count, depth_count, angle_count
    )
    total = spread[:, :, 0]
    for lag in range(1, depth_count):
        total = total.at[: depth_count - lag].add(spread[lag:, :, lag])
    return jnp.transpose(total, (1, 0, 2)) / math.sqrt(points)


def solution(mesh):
    placed = (
        P("depth", "freq", None, None, None),
        P("freq", None, None, None),
        P("freq", None, None, None),
        P(),
        P("freq"),
        P(),
    )
    return jax.shard_map(
        shards,
        mesh=mesh,
        in_specs=placed,
        out_specs=P(("freq", "depth"), None, None),
        check_vma=False,
    )
```

```python
import math

import jax
import jax.numpy as jnp
from jax import lax
from jax.experimental import pallas as pl
from jax.experimental.pallas import tpu as pltpu
from jax.sharding import PartitionSpec as P

CHUNKS = 8
GROUPS = (4, 2, 1, 1)

WHOLE = pl.BlockSpec(memory_space=pltpu.VMEM)
FAR = pl.BlockSpec(memory_space=pltpu.HBM)
LOOSE = pl.BlockSpec(memory_space=pl.ANY)


def first_round(level):
    return 3 * (level // 2) + level % 2


def handled(round_index, level, chunk_count):
    return 0 <= round_index - first_round(level) < chunk_count


def march(values, extrap_ref, out_ref):
    half = out_ref.shape[0] // 2
    real = jnp.dot(values, extrap_ref[0], preferred_element_type=jnp.float32)
    imag = jnp.dot(values, extrap_ref[1], preferred_element_type=jnp.float32)
    out_ref[:half] = (real[:half] - imag[half:]).astype(out_ref.dtype)
    out_ref[half:] = (imag[:half] + real[half:]).astype(out_ref.dtype)


def extend(arrived, extrap, order, above=None):
    rows, points = arrived.shape
    above = above or ()

    def kernel(arrived_ref, extrap_ref, order_ref, *refs):
        values = arrived_ref[...]
        if above:
            values = jnp.where(refs[1][...] > 0, refs[0][0], values)
        march(values, extrap_ref, refs[-1])

    return pl.pallas_call(
        kernel,
        out_shape=jax.ShapeDtypeStruct((rows, points), jnp.bfloat16),
        in_specs=[WHOLE, WHOLE, LOOSE] + [WHOLE] * len(above),
        out_specs=WHOLE,
        compiler_params=pltpu.CompilerParams(vmem_limit_bytes=12 << 20),
        cost_estimate=pl.CostEstimate(
            flops=4 * rows * points * points, bytes_accessed=4 * points * points, transcendentals=0
        ),
    )(arrived, extrap, order, *above)


def picked(shot_ref, source_ref, span, component):
    shot_count = source_ref.shape[0]
    count = span.stop - span.start
    pick = (
        shot_ref[span][None, :] == lax.broadcasted_iota(jnp.int32, (shot_count, count), 0)
    ).astype(jnp.bfloat16)
    return lax.dot_general(
        pick,
        source_ref[:, component, :],
        (((0,), (0,)), ((), ())),
        preferred_element_type=jnp.float32,
    ).astype(jnp.bfloat16)


def fill(out_ref, shot_ref, source_ref, record_ref, span):
    part = out_ref.shape[0] // 4
    out_ref[:part] = picked(shot_ref, source_ref, span, 0)
    out_ref[part : 2 * part] = record_ref[span, 1, :]
    out_ref[2 * part : 3 * part] = picked(shot_ref, source_ref, span, 1)
    out_ref[3 * part :] = record_ref[span, 0, :]


def head(extrap, sources, records, shots, part):
    points = extrap.shape[2]

    def kernel(
        extrap_hbm, source_hbm, record_hbm, shot_hbm, out_ref,
        extrap_ref, source_ref, record_ref, shot_ref, chunk_ref, sems,
    ):
        copies = [
            pltpu.make_async_copy(shot_hbm, shot_ref, sems.at[0]),
            pltpu.make_async_copy(source_hbm, source_ref, sems.at[1]),
            pltpu.make_async_copy(record_hbm.at[pl.ds(0, part)], record_ref, sems.at[2]),
            pltpu.make_async_copy(extrap_hbm, extrap_ref, sems.at[3]),
        ]
        for copy in copies:
            copy.start()
        for copy in copies[:3]:
            copy.wait()
        fill(chunk_ref, shot_ref, source_ref, record_ref, slice(0, part))
        copies[3].wait()
        march(chunk_ref[...], extrap_ref, out_ref)

    return pl.pallas_call(
        kernel,
        out_shape=jax.ShapeDtypeStruct((4 * part, points), jnp.bfloat16),
        in_specs=[FAR] * 4,
        out_specs=WHOLE,
        scratch_shapes=[
            pltpu.VMEM(extrap.shape, extrap.dtype),
            pltpu.VMEM(sources.shape, sources.dtype),
            pltpu.VMEM((part,) + records.shape[1:], records.dtype),
            pltpu.VMEM(shots.shape, shots.dtype),
            pltpu.VMEM((4 * part, points), jnp.bfloat16),
            pltpu.SemaphoreType.DMA((4,)),
        ],
        compiler_params=pltpu.CompilerParams(vmem_limit_bytes=56 << 20),
    )(extrap, sources, records, shots)


def surface(sources, records, shots, chunk_count):
    shot_count, _, points = sources.shape
    part = shot_count // chunk_count

    def kernel(source_ref, record_ref, shot_ref, out_ref):
        everything = slice(0, shot_count)
        for place, values in (
            (0, picked(shot_ref, source_ref, everything, 0)),
            (1, record_ref[:, 1, :]),
            (2, picked(shot_ref, source_ref, everything, 1)),
            (3, record_ref[:, 0, :]),
        ):
            for chunk in range(chunk_count):
                out_ref[chunk, place * part : (place + 1) * part] = values[
                    chunk * part : (chunk + 1) * part
                ]

    return pl.pallas_call(
        kernel,
        out_shape=jax.ShapeDtypeStruct((chunk_count, 4 * part, points), jnp.bfloat16),
        in_specs=[WHOLE] * 3,
        out_specs=WHOLE,
        compiler_params=pltpu.CompilerParams(vmem_limit_bytes=12 << 20),
    )(sources, records, shots)


def correlate(own, theirs, upper, own_scale, unit, part):
    points = own[0].shape[1]
    width = points // 2
    group_count = len(own)

    def stacks(ref, chunks, column):
        sources, records = [], []
        for chunk in range(chunks):
            row = 4 * part * chunk
            for first, second in ((0, 3), (2, 1)):
                sources.append(ref[row + first * part : row + (first + 1) * part, column])
                records.append(ref[row + second * part : row + (second + 1) * part, :])
        return sources, records

    def kernel(*refs):
        own_refs, their_refs = refs[:group_count], refs[group_count : 2 * group_count]
        upper_ref, own_scale_ref, out_ref = refs[2 * group_count :]
        note = own_refs[0].shape[0]
        their_scale = their_refs[0][note : note + 16, :128].astype(jnp.float32)[:1, :1] * unit

        def side(these, column):
            sources, records = [], []
            for ref, mine in zip(these, own_refs):
                first, second = stacks(ref, mine.shape[0] // (4 * part), column)
                sources += first
                records += second
            return lax.dot_general(
                jnp.concatenate(sources, axis=0),
                jnp.concatenate(records, axis=0),
                (((0,), (0,)), ((), ())),
                preferred_element_type=jnp.float32,
            )

        for value, column in ((0, slice(0, width)), (1, slice(width, points))):

            @pl.when(upper_ref[0] == value)
            def _():
                total = side(own_refs, column) * own_scale_ref[...]
                total += side(their_refs, column) * their_scale
                out_ref[...] = total.astype(out_ref.dtype)

    return pl.pallas_call(
        kernel,
        out_shape=jax.ShapeDtypeStruct((width, points), jnp.bfloat16),
        in_specs=[WHOLE] * (2 * group_count) + [pl.BlockSpec(memory_space=pltpu.SMEM)] + [WHOLE],
        out_specs=WHOLE,
        compiler_params=pltpu.CompilerParams(vmem_limit_bytes=24 << 20),
    )(*own, *theirs, upper, own_scale)


def angles(panel, angle_lag, depth_count):
    angle_count = angle_lag.shape[1]
    row_count = panel.shape[0] // depth_count
    points = panel.shape[1]

    def kernel(panel_ref, lag_ref, out_ref):
        total = None
        for lag in range(depth_count):
            column = (lag_ref[...] == lag).astype(jnp.bfloat16)
            skip = lag * row_count
            if row_count % 16 == 0:
                term = jnp.dot(panel_ref[skip:], column, preferred_element_type=jnp.float32)
            else:
                term = jnp.dot(panel_ref[...], column, preferred_element_type=jnp.float32)[skip:]
            if total is None:
                total = term
            elif skip:
                kept = total.shape[0] - skip
                total = jnp.concatenate([total[:kept] + term, total[kept:]], axis=0)
        total = total * (1.0 / math.sqrt(points))
        for depth in range(depth_count):
            out_ref[:, depth, :] = total[depth * row_count : (depth + 1) * row_count]

    return pl.pallas_call(
        kernel,
        out_shape=jax.ShapeDtypeStruct((row_count, depth_count, angle_count), jnp.float32),
        in_specs=[WHOLE] * 2,
        out_specs=WHOLE,
        compiler_params=pltpu.CompilerParams(vmem_limit_bytes=24 << 20),
    )(panel, angle_lag)


def shards(extrap, source_field, record_field, shot_of_record, freq_index, angle_lag):
    level = lax.axis_index("depth")
    depth_count = lax.axis_size("depth")
    freq_count = lax.axis_size("freq")
    freq_slot = lax.axis_index("freq")
    points = source_field.shape[3]
    shot_count = source_field.shape[1]
    chunk_count = CHUNKS
    part = shot_count // chunk_count
    rows = 4 * part

    operator = extrap[0, 0]
    sources, records = source_field[0], record_field[0]
    order = head(operator, sources, records, shot_of_record, part)
    above = surface(sources, records, shot_of_record, chunk_count)

    number = freq_index[0].astype(jnp.float32) + 1.0
    span = freq_count // 2
    upper = (freq_slot // span) % 2 == 1
    partner = [(slot, slot ^ span) for slot in range(freq_count)]

    at_surface = jnp.full((rows, points), level == 0).astype(jnp.bfloat16)
    my_first = 3 * (level // 2) + level % 2
    finished = jnp.zeros((chunk_count + 2, rows, points), jnp.bfloat16)
    sent = {}
    own, theirs = [], []
    start = 0
    round_count = first_round(depth_count - 1) + chunk_count
    for round_index in range(round_count):
        outcome = {}
        chunk = round_index - my_first
        for parity in (0, 1):
            levels = [
                z for z in range(parity, depth_count, 2) if handled(round_index, z, chunk_count)
            ]
            if not levels:
                continue
            if round_index or parity:
                arrived = sent.get((1 - parity, round_index - 2 + parity))
                entering = None
                if parity == 0 and round_index < chunk_count:
                    entering = (above[round_index : round_index + 1], at_surface)
                    if arrived is None:
                        arrived, entering = above[round_index], None
                order = extend(arrived, operator, order, entering)
            outcome[parity] = order
            pairs = [(z, z + 1) for z in levels if z + 1 < depth_count]
            if pairs:
                sent[parity, round_index] = lax.ppermute(order, "depth", pairs)
        if len(outcome) == 2:
            kept = jnp.where(level % 2 == 0, outcome[0], outcome[1])
        else:
            kept = next(iter(outcome.values()))
        slot = jnp.clip(chunk, -1, chunk_count) + 1
        finished = lax.dynamic_update_index_in_dim(finished, kept, slot, 0)
        size = GROUPS[len(own)] if len(own) < len(GROUPS) else 0
        if size and round_index - first_round(depth_count - 1) == start + size - 1:
            done = finished[1 + start : 1 + start + size].reshape(size * rows, points)
            own.append(done)
            payload = done
            if start == 0:
                note = jnp.full((16, points), number, jnp.float32).astype(jnp.bfloat16)
                payload = jnp.concatenate([done, note], axis=0)
            payload, order = lax.optimization_barrier((payload, order))
            received = lax.ppermute(payload, "freq", partner)
            theirs.append(received)
            start += size

    scale = 1.0 / (8 * freq_count) / math.sqrt(shot_count * freq_count)
    image = correlate(
        own,
        theirs,
        upper.astype(jnp.int32).reshape(1),
        (number * scale).reshape(1, 1),
        scale,
        part,
    )
    width = points // 2
    span //= 2
    while span:
        width //= 2
        upper = (freq_slot // span) % 2 == 1
        partner = [(slot, slot ^ span) for slot in range(freq_count)]
        keep = jnp.where(upper, image[width:], image[:width])
        away = jnp.where(upper, image[:width], image[width:])
        received = lax.ppermute(away, "freq", partner)
        image = (keep.astype(jnp.float32) + received.astype(jnp.float32)).astype(jnp.bfloat16)
        span //= 2
    panel = lax.all_to_all(image, "depth", split_axis=0, concat_axis=0, tiled=True)
    return angles(panel, angle_lag, depth_count)


def solution(mesh):
    placed = (
        P("depth", "freq", None, None, None),
        P("freq", None, None, None),
        P("freq", None, None, None),
        P(),
        P("freq"),
        P(),
    )
    return jax.shard_map(
        shards,
        mesh=mesh,
        in_specs=placed,
        out_specs=P(("freq", "depth"), None, None),
        check_vma=False,
    )
```

```python
import math

import jax
import jax.numpy as jnp
from jax import lax
from jax.experimental import pallas as pl
from jax.experimental.pallas import tpu as pltpu
from jax.sharding import PartitionSpec as P

CHUNKS = 8
GROUPS = (1,) * CHUNKS
LAGS = (3, 2)
TILES = 2

WHOLE = pl.BlockSpec(memory_space=pltpu.VMEM)
FAR = pl.BlockSpec(memory_space=pltpu.HBM)
BRIEF = pl.CostEstimate(flops=0, bytes_accessed=0, transcendentals=0)


def first_round(level):
    return sum(LAGS) * (level // 2) + LAGS[1] * (level % 2)


def handled(round_index, level, chunk_count):
    return 0 <= round_index - first_round(level) < chunk_count


def senders(round_index, parity, depth_count, chunk_count):
    everyone = list(range(parity, depth_count - 1, 2))
    levels = [level for level in everyone if handled(round_index, level, chunk_count)]
    if not levels or levels[0] == parity:
        return levels
    wanted = min(len(everyone), -(-chunk_count // sum(LAGS)))
    first, last = everyone.index(levels[0]), everyone.index(levels[-1])
    return everyone[first : max(first + wanted, last + 1)]


def march(values, extrap_ref, out_ref):
    half = out_ref.shape[0] // 2
    points = out_ref.shape[1]
    width = points // TILES

    @pl.loop(0, TILES)
    def _(tile):
        column = pl.ds(pl.multiple_of(tile * width, width), width)
        real = jnp.dot(values, extrap_ref[0, :, column], preferred_element_type=jnp.float32)
        imag = jnp.dot(values, extrap_ref[1, :, column], preferred_element_type=jnp.float32)
        out_ref[:half, column] = (real[:half] - imag[half:]).astype(out_ref.dtype)
        out_ref[half:, column] = (imag[:half] + real[half:]).astype(out_ref.dtype)


def extend(arrived, extrap, finished, round_index, parity, above, sends):
    rows, points = arrived.shape
    chunk_count = finished.shape[0]

    def kernel(arrived_ref, extrap_ref, finished_in, *refs):
        finished_ref = refs[-1]
        level = lax.axis_index("depth")
        chunk = round_index - first_round(level)
        mine = (level % 2 == parity) & (chunk >= 0) & (chunk < chunk_count)
        place_ref = finished_ref.at[jnp.clip(chunk, 0, chunk_count - 1)]
        out_ref = refs[-2] if sends else place_ref
        if above:

            @pl.when(level == 0)
            def _():
                march(refs[0][0], extrap_ref, out_ref)

        @pl.when(mine & ((level > 0) | (not above)))
        def _():
            march(arrived_ref[...], extrap_ref, out_ref)

        if sends:

            @pl.when(mine)
            def _():
                place_ref[...] = out_ref[...]

    kept = jax.ShapeDtypeStruct(finished.shape, finished.dtype)
    sent = jax.ShapeDtypeStruct((rows, points), jnp.bfloat16)
    return pl.pallas_call(
        kernel,
        out_shape=[sent, kept] if sends else [kept],
        in_specs=[WHOLE, WHOLE, WHOLE] + [WHOLE] * len(above),
        out_specs=[WHOLE, WHOLE] if sends else [WHOLE],
        input_output_aliases={2: 1 if sends else 0},
        compiler_params=pltpu.CompilerParams(vmem_limit_bytes=8 << 20),
        cost_estimate=BRIEF,
    )(arrived, extrap, finished, *above)


def pack(finished, number, start, stop, noted):
    rows, points = finished.shape[1:]
    part = rows // 4
    half = points // 2
    count = 2 * part * (stop - start)

    def kernel(finished_ref, number_ref, out_ref):
        span = lax.axis_size("freq") // 2
        upper = (lax.axis_index("freq") // span) % 2
        column = pl.ds(pl.multiple_of((1 - upper) * half, half), half)
        for chunk in range(start, stop):
            for index, (first, second) in enumerate(((0, 3), (2, 1))):
                row = pl.ds((2 * (chunk - start) + index) * part, part)
                out_ref[row, :points] = finished_ref[chunk, pl.ds(second * part, part), :]
                out_ref[row, points:] = finished_ref[chunk, pl.ds(first * part, part), column]
        if noted:
            out_ref[count:] = jnp.broadcast_to(
                number_ref[...].astype(out_ref.dtype), (16, out_ref.shape[1])
            )

    return pl.pallas_call(
        kernel,
        out_shape=jax.ShapeDtypeStruct((count + 16 * noted, points + half), jnp.bfloat16),
        in_specs=[WHOLE] * 2,
        out_specs=WHOLE,
        compiler_params=pltpu.CompilerParams(vmem_limit_bytes=8 << 20),
        cost_estimate=BRIEF,
    )(finished, number)


def picked(shot_ref, source_ref, span, component):
    shot_count = source_ref.shape[0]
    count = span.stop - span.start
    pick = (
        shot_ref[span][None, :] == lax.broadcasted_iota(jnp.int32, (shot_count, count), 0)
    ).astype(jnp.bfloat16)
    return lax.dot_general(
        pick,
        source_ref[:, component, :],
        (((0,), (0,)), ((), ())),
        preferred_element_type=jnp.float32,
    ).astype(jnp.bfloat16)


def fill(out_ref, shot_ref, source_ref, record_ref, span):
    part = out_ref.shape[0] // 4
    out_ref[:part] = picked(shot_ref, source_ref, span, 0)
    out_ref[part : 2 * part] = record_ref[span, 1, :]
    out_ref[2 * part : 3 * part] = picked(shot_ref, source_ref, span, 1)
    out_ref[3 * part :] = record_ref[span, 0, :]


def head(extrap, sources, records, shots, part):
    points = extrap.shape[2]

    def kernel(
        extrap_hbm, source_hbm, record_hbm, shot_hbm, out_ref,
        extrap_ref, source_ref, record_ref, shot_ref, chunk_ref, sems,
    ):
        copies = [
            pltpu.make_async_copy(shot_hbm, shot_ref, sems.at[0]),
            pltpu.make_async_copy(source_hbm, source_ref, sems.at[1]),
            pltpu.make_async_copy(record_hbm.at[pl.ds(0, part)], record_ref, sems.at[2]),
            pltpu.make_async_copy(extrap_hbm, extrap_ref, sems.at[3]),
        ]
        for copy in copies:
            copy.start()
        for copy in copies[:3]:
            copy.wait()
        fill(chunk_ref, shot_ref, source_ref, record_ref, slice(0, part))
        copies[3].wait()
        march(chunk_ref[...], extrap_ref, out_ref)

    return pl.pallas_call(
        kernel,
        out_shape=jax.ShapeDtypeStruct((4 * part, points), jnp.bfloat16),
        in_specs=[FAR] * 4,
        out_specs=WHOLE,
        scratch_shapes=[
            pltpu.VMEM(extrap.shape, extrap.dtype),
            pltpu.VMEM(sources.shape, sources.dtype),
            pltpu.VMEM((part,) + records.shape[1:], records.dtype),
            pltpu.VMEM(shots.shape, shots.dtype),
            pltpu.VMEM((4 * part, points), jnp.bfloat16),
            pltpu.SemaphoreType.DMA((4,)),
        ],
        compiler_params=pltpu.CompilerParams(vmem_limit_bytes=56 << 20),
    )(extrap, sources, records, shots)


def surface(sources, records, shots, chunk_count, first):
    shot_count, _, points = sources.shape
    part = shot_count // chunk_count

    def kernel(source_ref, record_ref, shot_ref, first_ref, out_ref, finished_ref):
        finished_ref[0] = first_ref[...]
        everything = slice(0, shot_count)
        for place, values in (
            (0, picked(shot_ref, source_ref, everything, 0)),
            (1, record_ref[:, 1, :]),
            (2, picked(shot_ref, source_ref, everything, 1)),
            (3, record_ref[:, 0, :]),
        ):
            for chunk in range(chunk_count):
                out_ref[chunk, place * part : (place + 1) * part] = values[
                    chunk * part : (chunk + 1) * part
                ]

    return pl.pallas_call(
        kernel,
        out_shape=[jax.ShapeDtypeStruct((chunk_count, 4 * part, points), jnp.bfloat16)] * 2,
        in_specs=[WHOLE] * 4,
        out_specs=[WHOLE] * 2,
        compiler_params=pltpu.CompilerParams(vmem_limit_bytes=12 << 20),
    )(sources, records, shots, first)


def correlate(finished, theirs, own_scale, unit, part):
    points = finished.shape[2]
    chunk_count = finished.shape[0]
    width = points // 2
    depth = 2 * chunk_count * part

    def kernel(finished_ref, *refs):
        their_refs = refs[: len(theirs)]
        scale_ref, out_ref, source_ref, record_ref = refs[len(theirs) :]
        span = lax.axis_size("freq") // 2
        upper = (lax.axis_index("freq") // span) % 2
        column = pl.ds(pl.multiple_of(upper * width, width), width)

        def product():
            return lax.dot_general(
                source_ref[...],
                record_ref[...],
                (((0,), (0,)), ((), ())),
                preferred_element_type=jnp.float32,
            )

        for chunk in range(chunk_count):
            for index, (first, second) in enumerate(((0, 3), (2, 1))):
                row = pl.ds((2 * chunk + index) * part, part)
                source_ref[row] = finished_ref[chunk, pl.ds(first * part, part), column]
                record_ref[row] = finished_ref[chunk, pl.ds(second * part, part), :]
        total = product() * scale_ref[...]
        start = 0
        for group, ref in zip(GROUPS, their_refs):
            count = 2 * group * part
            source_ref[start : start + count] = ref[:count, points:]
            record_ref[start : start + count] = ref[:count, :points]
            start += count
        count = 2 * GROUPS[0] * part
        number = their_refs[0][count : count + 16, :128].astype(jnp.float32)[:1, :1]
        total += product() * (number * unit)
        out_ref[...] = total.astype(out_ref.dtype)

    return pl.pallas_call(
        kernel,
        out_shape=jax.ShapeDtypeStruct((width, points), jnp.bfloat16),
        in_specs=[WHOLE] * (2 + len(theirs)),
        out_specs=WHOLE,
        scratch_shapes=[
            pltpu.VMEM((depth, width), jnp.bfloat16),
            pltpu.VMEM((depth, points), jnp.bfloat16),
        ],
        compiler_params=pltpu.CompilerParams(vmem_limit_bytes=24 << 20),
    )(finished, *theirs, own_scale)


def angles(panel, angle_lag, depth_count):
    angle_count = angle_lag.shape[1]
    row_count = panel.shape[0] // depth_count
    points = panel.shape[1]

    def kernel(panel_ref, lag_ref, out_ref):
        total = None
        for lag in range(depth_count):
            column = (lag_ref[...] == lag).astype(jnp.bfloat16)
            skip = lag * row_count
            if row_count % 16 == 0:
                term = jnp.dot(panel_ref[skip:], column, preferred_element_type=jnp.float32)
            else:
                term = jnp.dot(panel_ref[...], column, preferred_element_type=jnp.float32)[skip:]
            if total is None:
                total = term
            elif skip:
                kept = total.shape[0] - skip
                total = jnp.concatenate([total[:kept] + term, total[kept:]], axis=0)
        total = total * (1.0 / math.sqrt(points))
        for depth in range(depth_count):
            out_ref[:, depth, :] = total[depth * row_count : (depth + 1) * row_count]

    return pl.pallas_call(
        kernel,
        out_shape=jax.ShapeDtypeStruct((row_count, depth_count, angle_count), jnp.float32),
        in_specs=[WHOLE] * 2,
        out_specs=WHOLE,
        compiler_params=pltpu.CompilerParams(vmem_limit_bytes=24 << 20),
    )(panel, angle_lag)


def shards(extrap, source_field, record_field, shot_of_record, freq_index, angle_lag):
    depth_count = lax.axis_size("depth")
    freq_count = lax.axis_size("freq")
    freq_slot = lax.axis_index("freq")
    points = source_field.shape[3]
    shot_count = source_field.shape[1]
    chunk_count = CHUNKS
    part = shot_count // chunk_count

    operator = extrap[0, 0]
    sources, records = source_field[0], record_field[0]
    order = [head(operator, sources, records, shot_of_record, part)]
    above, finished = surface(sources, records, shot_of_record, chunk_count, order[0])

    number = freq_index[0].astype(jnp.float32).reshape(1, 1) + 1.0
    span = freq_count // 2
    partner = [(slot, slot ^ span) for slot in range(freq_count)]

    sent = {}
    theirs = []
    round_count = first_round(depth_count - 1) + chunk_count
    for round_index in range(round_count):
        for parity in (0, 1):
            levels = [
                z for z in range(parity, depth_count, 2) if handled(round_index, z, chunk_count)
            ]
            if not levels:
                continue
            pairs = [(z, z + 1) for z in senders(round_index, parity, depth_count, chunk_count)]
            if round_index or parity:
                arrived = sent.get((1 - parity, round_index - LAGS[parity]))
                entering = ()
                if parity == 0 and round_index < chunk_count:
                    entering = (above[round_index : round_index + 1],)
                    if arrived is None:
                        arrived, entering = above[round_index], ()
                *order, finished = extend(
                    arrived, operator, finished, round_index, parity, entering, bool(pairs)
                )
            if pairs:
                sent[parity, round_index] = lax.ppermute(order[0], "depth", pairs)
        stop = sum(GROUPS[: len(theirs) + 1])
        if len(theirs) < len(GROUPS) and round_index - first_round(depth_count - 1) == stop - 1:
            start = stop - GROUPS[len(theirs)]
            payload = pack(finished, number, start, stop, start == 0)
            payload, finished = lax.optimization_barrier((payload, finished))
            theirs.append(lax.ppermute(payload, "freq", partner))

    scale = 1.0 / (8 * freq_count) / math.sqrt(shot_count * freq_count)
    image = correlate(finished, theirs, number * scale, scale, part)
    width = points // 2
    span //= 2
    while span:
        width //= 2
        upper = (freq_slot // span) % 2 == 1
        partner = [(slot, slot ^ span) for slot in range(freq_count)]
        keep = jnp.where(upper, image[width:], image[:width])
        away = jnp.where(upper, image[:width], image[width:])
        received = lax.ppermute(away, "freq", partner)
        image = (keep.astype(jnp.float32) + received.astype(jnp.float32)).astype(jnp.bfloat16)
        span //= 2
    panel = lax.all_to_all(image, "depth", split_axis=0, concat_axis=0, tiled=True)
    return angles(panel, angle_lag, depth_count)


def solution(mesh):
    placed = (
        P("depth", "freq", None, None, None),
        P("freq", None, None, None),
        P("freq", None, None, None),
        P(),
        P("freq"),
        P(),
    )
    return jax.shard_map(
        shards,
        mesh=mesh,
        in_specs=placed,
        out_specs=P(("freq", "depth"), None, None),
        check_vma=False,
    )
```

```python
import math

import jax
import jax.numpy as jnp
from jax import lax
from jax.experimental import pallas as pl
from jax.experimental.pallas import tpu as pltpu
from jax.sharding import PartitionSpec as P

CHUNKS = 8
GROUPS = (3, 2, 2, 1)
LAGS = (3, 2)
EARLY = LAGS[1]

WHOLE = pl.BlockSpec(memory_space=pltpu.VMEM)
FAR = pl.BlockSpec(memory_space=pltpu.HBM)
BRIEF = pl.CostEstimate(flops=0, bytes_accessed=0, transcendentals=0)


def first_round(level):
    return sum(LAGS) * (level // 2) + LAGS[1] * (level % 2)


def handled(round_index, level, chunk_count):
    return 0 <= round_index - first_round(level) < chunk_count


def senders(round_index, parity, depth_count, chunk_count):
    everyone = list(range(parity, depth_count - 1, 2))
    levels = [level for level in everyone if handled(round_index, level, chunk_count)]
    if not levels or levels[0] == parity:
        return levels
    wanted = min(len(everyone), -(-chunk_count // sum(LAGS)))
    first, last = everyone.index(levels[0]), everyone.index(levels[-1])
    return everyone[first : max(first + wanted, last + 1)]


def march(values, extrap_ref, out_refs):
    rows = out_refs[0].shape[0]
    half = rows // 2
    real = jnp.dot(values, extrap_ref[0], preferred_element_type=jnp.float32)
    imag = jnp.dot(values, extrap_ref[1], preferred_element_type=jnp.float32)
    for chunk, out_ref in enumerate(out_refs):
        upper = slice(chunk * rows, chunk * rows + half)
        lower = slice(chunk * rows + half, (chunk + 1) * rows)
        out_ref[:half] = (real[upper] - imag[lower]).astype(out_ref.dtype)
        out_ref[half:] = (imag[upper] + real[lower]).astype(out_ref.dtype)


def extend(arrived, extrap, finished, round_index, parity, sends):
    rows, points = arrived.shape
    chunk_count = finished.shape[0]

    def kernel(arrived_ref, extrap_ref, finished_in, *refs):
        finished_ref = refs[-1]
        level = lax.axis_index("depth")
        chunk = round_index - first_round(level)
        mine = (level > 0) & (level % 2 == parity) & (chunk >= 0) & (chunk < chunk_count)
        place_ref = finished_ref.at[jnp.clip(chunk, 0, chunk_count - 1)]
        out_ref = refs[-2] if sends else place_ref

        @pl.when(mine)
        def _():
            march(arrived_ref[...], extrap_ref, [out_ref])

        if sends:

            @pl.when(mine)
            def _():
                place_ref[...] = out_ref[...]

            if parity == 0 and round_index < chunk_count:

                @pl.when(level == 0)
                def _():
                    out_ref[...] = finished_ref[round_index]

    kept = jax.ShapeDtypeStruct(finished.shape, finished.dtype)
    sent = jax.ShapeDtypeStruct((rows, points), jnp.bfloat16)
    return pl.pallas_call(
        kernel,
        out_shape=[sent, kept] if sends else [kept],
        in_specs=[WHOLE, WHOLE, WHOLE],
        out_specs=[WHOLE, WHOLE] if sends else [WHOLE],
        input_output_aliases={2: 1 if sends else 0},
        compiler_params=pltpu.CompilerParams(vmem_limit_bytes=8 << 20),
        cost_estimate=BRIEF,
    )(arrived, extrap, finished)


def pack(finished, number, start, stop, noted):
    rows, points = finished.shape[1:]
    part = rows // 4
    half = points // 2
    count = 2 * part * (stop - start)

    def kernel(finished_ref, number_ref, out_ref):
        span = lax.axis_size("freq") // 2
        upper = (lax.axis_index("freq") // span) % 2
        column = pl.ds(pl.multiple_of((1 - upper) * half, half), half)
        for chunk in range(start, stop):
            for index, (first, second) in enumerate(((0, 3), (2, 1))):
                row = pl.ds((2 * (chunk - start) + index) * part, part)
                out_ref[row, :points] = finished_ref[chunk, pl.ds(second * part, part), :]
                out_ref[row, points:] = finished_ref[chunk, pl.ds(first * part, part), column]
        if noted:
            out_ref[count:] = jnp.broadcast_to(
                number_ref[...].astype(out_ref.dtype), (16, out_ref.shape[1])
            )

    return pl.pallas_call(
        kernel,
        out_shape=jax.ShapeDtypeStruct((count + 16 * noted, points + half), jnp.bfloat16),
        in_specs=[WHOLE] * 2,
        out_specs=WHOLE,
        compiler_params=pltpu.CompilerParams(vmem_limit_bytes=8 << 20),
        cost_estimate=BRIEF,
    )(finished, number)


def fill(out_ref, shot_ref, source_ref, record_ref, first, part):
    shot_count = source_ref.shape[0]
    chunk_count = out_ref.shape[0] // (4 * part)
    pick = (
        shot_ref[...][None, :] == lax.broadcasted_iota(jnp.int32, (shot_count, shot_count), 0)
    ).astype(jnp.bfloat16)

    def picked(component):
        return lax.dot_general(
            pick,
            source_ref[:, component, :],
            (((0,), (0,)), ((), ())),
            preferred_element_type=jnp.float32,
        ).astype(jnp.bfloat16)

    for place, values in (
        (0, picked(0)),
        (1, record_ref[:, 1, :]),
        (2, picked(1)),
        (3, record_ref[:, 0, :]),
    ):
        for chunk in range(chunk_count):
            row = (4 * chunk + place) * part
            shot = (first + chunk) * part
            out_ref[row : row + part] = values[shot : shot + part]


def head(extrap, sources, records, shots, part):
    points = extrap.shape[2]
    rows = 4 * part

    def kernel(extrap_hbm, source_hbm, record_hbm, shot_hbm, *refs):
        out_refs = refs[:EARLY]
        extrap_ref, source_ref, record_ref, shot_ref, chunk_ref, sems = refs[EARLY:]

        @pl.when(lax.axis_index("depth") == 0)
        def _():
            copies = [
                pltpu.make_async_copy(shot_hbm, shot_ref, sems.at[0]),
                pltpu.make_async_copy(source_hbm, source_ref, sems.at[1]),
                pltpu.make_async_copy(record_hbm.at[pl.ds(0, EARLY * part)], record_ref, sems.at[2]),
                pltpu.make_async_copy(extrap_hbm, extrap_ref, sems.at[3]),
            ]
            for copy in copies:
                copy.start()
            for copy in copies[:3]:
                copy.wait()
            fill(chunk_ref, shot_ref, source_ref, record_ref, 0, part)
            copies[3].wait()
            march(chunk_ref[...], extrap_ref, out_refs)

    return pl.pallas_call(
        kernel,
        out_shape=[jax.ShapeDtypeStruct((rows, points), jnp.bfloat16)] * EARLY,
        in_specs=[FAR] * 4,
        out_specs=[WHOLE] * EARLY,
        scratch_shapes=[
            pltpu.VMEM(extrap.shape, extrap.dtype),
            pltpu.VMEM(sources.shape, sources.dtype),
            pltpu.VMEM((EARLY * part,) + records.shape[1:], records.dtype),
            pltpu.VMEM(shots.shape, shots.dtype),
            pltpu.VMEM((EARLY * rows, points), jnp.bfloat16),
            pltpu.SemaphoreType.DMA((4,)),
        ],
        compiler_params=pltpu.CompilerParams(vmem_limit_bytes=56 << 20),
    )(extrap, sources, records, shots)


def rest(extrap, sources, records, shots, firsts, chunk_count):
    shot_count, _, points = sources.shape
    part = shot_count // chunk_count
    rows = 4 * part

    def kernel(extrap_ref, source_ref, record_ref, shot_ref, *refs):
        first_refs = refs[: len(firsts)]
        finished_ref, chunk_ref = refs[len(firsts) :]

        @pl.when(lax.axis_index("depth") == 0)
        def _():
            fill(chunk_ref, shot_ref, source_ref, record_ref, len(firsts), part)
            others = [finished_ref.at[chunk] for chunk in range(len(firsts), chunk_count)]
            march(chunk_ref[...], extrap_ref, others)
            for chunk, first_ref in enumerate(first_refs):
                finished_ref[chunk] = first_ref[...]

    return pl.pallas_call(
        kernel,
        out_shape=jax.ShapeDtypeStruct((chunk_count, rows, points), jnp.bfloat16),
        in_specs=[WHOLE] * (4 + len(firsts)),
        out_specs=WHOLE,
        scratch_shapes=[pltpu.VMEM(((chunk_count - len(firsts)) * rows, points), jnp.bfloat16)],
        compiler_params=pltpu.CompilerParams(vmem_limit_bytes=16 << 20),
        cost_estimate=BRIEF,
    )(extrap, sources, records, shots, *firsts)


def correlate(finished, theirs, own_scale, unit, part):
    points = finished.shape[2]
    chunk_count = finished.shape[0]
    width = points // 2
    depth = 2 * chunk_count * part

    def kernel(finished_ref, *refs):
        their_refs = refs[: len(theirs)]
        scale_ref, out_ref, source_ref, record_ref = refs[len(theirs) :]
        span = lax.axis_size("freq") // 2
        upper = (lax.axis_index("freq") // span) % 2
        column = pl.ds(pl.multiple_of(upper * width, width), width)

        def product():
            return lax.dot_general(
                source_ref[...],
                record_ref[...],
                (((0,), (0,)), ((), ())),
                preferred_element_type=jnp.float32,
            )

        for chunk in range(chunk_count):
            for index, (first, second) in enumerate(((0, 3), (2, 1))):
                row = pl.ds((2 * chunk + index) * part, part)
                source_ref[row] = finished_ref[chunk, pl.ds(first * part, part), column]
                record_ref[row] = finished_ref[chunk, pl.ds(second * part, part), :]
        total = product() * scale_ref[...]
        start = 0
        for group, ref in zip(GROUPS, their_refs):
            count = 2 * group * part
            source_ref[start : start + count] = ref[:count, points:]
            record_ref[start : start + count] = ref[:count, :points]
            start += count
        count = 2 * GROUPS[0] * part
        number = their_refs[0][count : count + 16, :128].astype(jnp.float32)[:1, :1]
        total += product() * (number * unit)
        out_ref[...] = total.astype(out_ref.dtype)

    return pl.pallas_call(
        kernel,
        out_shape=jax.ShapeDtypeStruct((width, points), jnp.bfloat16),
        in_specs=[WHOLE] * (2 + len(theirs)),
        out_specs=WHOLE,
        scratch_shapes=[
            pltpu.VMEM((depth, width), jnp.bfloat16),
            pltpu.VMEM((depth, points), jnp.bfloat16),
        ],
        compiler_params=pltpu.CompilerParams(vmem_limit_bytes=24 << 20),
    )(finished, *theirs, own_scale)


def angles(panel, angle_lag, depth_count):
    angle_count = angle_lag.shape[1]
    row_count = panel.shape[0] // depth_count
    points = panel.shape[1]

    def kernel(panel_ref, lag_ref, out_ref):
        total = None
        for lag in range(depth_count):
            column = (lag_ref[...] == lag).astype(jnp.bfloat16)
            skip = lag * row_count
            if row_count % 16 == 0:
                term = jnp.dot(panel_ref[skip:], column, preferred_element_type=jnp.float32)
            else:
                term = jnp.dot(panel_ref[...], column, preferred_element_type=jnp.float32)[skip:]
            if total is None:
                total = term
            elif skip:
                kept = total.shape[0] - skip
                total = jnp.concatenate([total[:kept] + term, total[kept:]], axis=0)
        total = total * (1.0 / math.sqrt(points))
        for depth in range(depth_count):
            out_ref[:, depth, :] = total[depth * row_count : (depth + 1) * row_count]

    return pl.pallas_call(
        kernel,
        out_shape=jax.ShapeDtypeStruct((row_count, depth_count, angle_count), jnp.float32),
        in_specs=[WHOLE] * 2,
        out_specs=WHOLE,
        compiler_params=pltpu.CompilerParams(vmem_limit_bytes=24 << 20),
    )(panel, angle_lag)


def shards(extrap, source_field, record_field, shot_of_record, freq_index, angle_lag):
    depth_count = lax.axis_size("depth")
    freq_count = lax.axis_size("freq")
    freq_slot = lax.axis_index("freq")
    points = source_field.shape[3]
    shot_count = source_field.shape[1]
    chunk_count = CHUNKS
    part = shot_count // chunk_count

    operator = extrap[0, 0]
    sources, records = source_field[0], record_field[0]
    firsts = head(operator, sources, records, shot_of_record, part)

    number = freq_index[0].astype(jnp.float32).reshape(1, 1) + 1.0
    span = freq_count // 2
    partner = [(slot, slot ^ span) for slot in range(freq_count)]

    sent = {}
    theirs = []
    round_count = first_round(depth_count - 1) + chunk_count
    for round_index in range(round_count):
        if round_index == EARLY:
            finished = rest(operator, sources, records, shot_of_record, firsts, chunk_count)
        for parity in (0, 1):
            if not any(
                handled(round_index, level, chunk_count)
                for level in range(parity, depth_count, 2)
            ):
                continue
            pairs = [
                (level, level + 1)
                for level in senders(round_index, parity, depth_count, chunk_count)
            ]
            if round_index < EARLY:
                order = firsts[round_index]
            else:
                arrived = sent.get((1 - parity, round_index - LAGS[parity]), firsts[0])
                *order, finished = extend(
                    arrived, operator, finished, round_index, parity, bool(pairs)
                )
                order = order[0] if pairs else None
            if pairs:
                sent[parity, round_index] = lax.ppermute(order, "depth", pairs)
        stop = sum(GROUPS[: len(theirs) + 1])
        if len(theirs) < len(GROUPS) and round_index - first_round(depth_count - 1) == stop - 1:
            start = stop - GROUPS[len(theirs)]
            payload = pack(finished, number, start, stop, start == 0)
            payload, finished = lax.optimization_barrier((payload, finished))
            theirs.append(lax.ppermute(payload, "freq", partner))

    scale = 1.0 / (8 * freq_count) / math.sqrt(shot_count * freq_count)
    image = correlate(finished, theirs, number * scale, scale, part)
    width = points // 2
    span //= 2
    while span:
        width //= 2
        upper = (freq_slot // span) % 2 == 1
        partner = [(slot, slot ^ span) for slot in range(freq_count)]
        keep = jnp.where(upper, image[width:], image[:width])
        away = jnp.where(upper, image[:width], image[width:])
        received = lax.ppermute(away, "freq", partner)
        image = (keep.astype(jnp.float32) + received.astype(jnp.float32)).astype(jnp.bfloat16)
        span //= 2
    panel = lax.all_to_all(image, "depth", split_axis=0, concat_axis=0, tiled=True)
    return angles(panel, angle_lag, depth_count)


def solution(mesh):
    placed = (
        P("depth", "freq", None, None, None),
        P("freq", None, None, None),
        P("freq", None, None, None),
        P(),
        P("freq"),
        P(),
    )
    return jax.shard_map(
        shards,
        mesh=mesh,
        in_specs=placed,
        out_specs=P(("freq", "depth"), None, None),
        check_vma=False,
    )
```

```python
import math

import jax
import jax.numpy as jnp
from jax import lax
from jax.experimental import pallas as pl
from jax.experimental.pallas import tpu as pltpu
from jax.sharding import PartitionSpec as P

CHUNKS = 8
GROUPS = (3, 2, 2, 1)
LAGS = (3, 2)
EARLY = LAGS[1]
SLICES = 2

WHOLE = pl.BlockSpec(memory_space=pltpu.VMEM)
FAR = pl.BlockSpec(memory_space=pltpu.HBM)
BRIEF = pl.CostEstimate(flops=0, bytes_accessed=0, transcendentals=0)


def first_round(level):
    return sum(LAGS) * (level // 2) + LAGS[1] * (level % 2)


def handled(round_index, level, chunk_count):
    return 0 <= round_index - first_round(level) < chunk_count


def senders(round_index, parity, depth_count, chunk_count):
    everyone = list(range(parity, depth_count - 1, 2))
    levels = [level for level in everyone if handled(round_index, level, chunk_count)]
    if not levels or levels[0] == parity:
        return levels
    wanted = min(len(everyone), -(-chunk_count // sum(LAGS)))
    first, last = everyone.index(levels[0]), everyone.index(levels[-1])
    return everyone[first : max(first + wanted, last + 1)]


def march(values, extrap_ref, out_refs):
    real = jnp.dot(values, extrap_ref[0], preferred_element_type=jnp.float32)
    imag = jnp.dot(values, extrap_ref[1], preferred_element_type=jnp.float32)
    combine(real, imag, out_refs)


def combine(real, imag, out_refs):
    rows = out_refs[0].shape[0]
    half = rows // 2
    for chunk, out_ref in enumerate(out_refs):
        upper = slice(chunk * rows, chunk * rows + half)
        lower = slice(chunk * rows + half, (chunk + 1) * rows)
        out_ref[:half] = (real[upper] - imag[lower]).astype(out_ref.dtype)
        out_ref[half:] = (imag[upper] + real[lower]).astype(out_ref.dtype)


def extend(arrived, extrap, finished, round_index, parity, sends, first=()):
    rows, points = arrived.shape
    chunk_count = finished.shape[0]

    def kernel(arrived_ref, extrap_ref, finished_in, *refs):
        finished_ref = refs[-1]
        level = lax.axis_index("depth")
        chunk = round_index - first_round(level)
        mine = (level > 0) & (level % 2 == parity) & (chunk >= 0) & (chunk < chunk_count)
        place_ref = finished_ref.at[jnp.clip(chunk, 0, chunk_count - 1)]
        out_ref = refs[-2] if sends else place_ref

        @pl.when(mine)
        def _():
            march(arrived_ref[...], extrap_ref, [out_ref])

        if sends:

            @pl.when(mine)
            def _():
                place_ref[...] = out_ref[...]

            if parity == 0 and round_index < chunk_count:

                @pl.when(level == 0)
                def _():
                    out_ref[...] = finished_ref[round_index]
                    if first:
                        finished_ref[round_index - EARLY] = refs[0][...]

    kept = jax.ShapeDtypeStruct(finished.shape, finished.dtype)
    sent = jax.ShapeDtypeStruct((rows, points), jnp.bfloat16)
    return pl.pallas_call(
        kernel,
        out_shape=[sent, kept] if sends else [kept],
        in_specs=[WHOLE] * (3 + len(first)),
        out_specs=[WHOLE, WHOLE] if sends else [WHOLE],
        input_output_aliases={2: 1 if sends else 0},
        compiler_params=pltpu.CompilerParams(vmem_limit_bytes=8 << 20),
        cost_estimate=BRIEF,
    )(arrived, extrap, finished, *first)


def pack(finished, number, start, stop, noted):
    rows, points = finished.shape[1:]
    part = rows // 4
    half = points // 2
    count = 2 * part * (stop - start)

    def kernel(finished_ref, number_ref, out_ref):
        span = lax.axis_size("freq") // 2
        upper = (lax.axis_index("freq") // span) % 2
        column = pl.ds(pl.multiple_of((1 - upper) * half, half), half)
        for chunk in range(start, stop):
            for index, (first, second) in enumerate(((0, 3), (2, 1))):
                row = pl.ds((2 * (chunk - start) + index) * part, part)
                out_ref[row, :points] = finished_ref[chunk, pl.ds(second * part, part), :]
                out_ref[row, points:] = finished_ref[chunk, pl.ds(first * part, part), column]
        if noted:
            out_ref[count:] = jnp.broadcast_to(
                number_ref[...].astype(out_ref.dtype), (16, out_ref.shape[1])
            )

    return pl.pallas_call(
        kernel,
        out_shape=jax.ShapeDtypeStruct((count + 16 * noted, points + half), jnp.bfloat16),
        in_specs=[WHOLE] * 2,
        out_specs=WHOLE,
        compiler_params=pltpu.CompilerParams(vmem_limit_bytes=8 << 20),
        cost_estimate=BRIEF,
    )(finished, number)


def fill(out_ref, shot_ref, source_ref, record_ref, first, part):
    shot_count = source_ref.shape[0]
    chunk_count = out_ref.shape[0] // (4 * part)
    pick = (
        shot_ref[...][None, :] == lax.broadcasted_iota(jnp.int32, (shot_count, shot_count), 0)
    ).astype(jnp.bfloat16)

    def picked(component):
        return lax.dot_general(
            pick,
            source_ref[:, component, :],
            (((0,), (0,)), ((), ())),
            preferred_element_type=jnp.float32,
        ).astype(jnp.bfloat16)

    for place, values in (
        (0, picked(0)),
        (1, record_ref[:, 1, :]),
        (2, picked(1)),
        (3, record_ref[:, 0, :]),
    ):
        for chunk in range(chunk_count):
            row = (4 * chunk + place) * part
            shot = (first + chunk) * part
            out_ref[row : row + part] = values[shot : shot + part]


def head(extrap, sources, records, shots, part):
    points = extrap.shape[2]
    rows = 4 * part

    def kernel(extrap_hbm, source_hbm, record_hbm, shot_hbm, *refs):
        out_refs = refs[:EARLY]
        extrap_ref, source_ref, record_ref, shot_ref, chunk_ref, sems = refs[EARLY:]

        @pl.when(lax.axis_index("depth") == 0)
        def _():
            copies = [
                pltpu.make_async_copy(shot_hbm, shot_ref, sems.at[0]),
                pltpu.make_async_copy(source_hbm, source_ref, sems.at[1]),
                pltpu.make_async_copy(record_hbm.at[pl.ds(0, EARLY * part)], record_ref, sems.at[2]),
            ]
            bands = [pl.ds(index * points // SLICES, points // SLICES) for index in range(SLICES)]
            copies += [
                pltpu.make_async_copy(
                    extrap_hbm.at[:, band], extrap_ref.at[:, band], sems.at[3 + index]
                )
                for index, band in enumerate(bands)
            ]
            for copy in copies:
                copy.start()
            for copy in copies[:3]:
                copy.wait()
            fill(chunk_ref, shot_ref, source_ref, record_ref, 0, part)
            real = imag = 0.0
            for copy, band in zip(copies[3:], bands):
                copy.wait()
                values = chunk_ref[:, band]
                real += jnp.dot(values, extrap_ref[0, band], preferred_element_type=jnp.float32)
                imag += jnp.dot(values, extrap_ref[1, band], preferred_element_type=jnp.float32)
            combine(real, imag, out_refs)

    return pl.pallas_call(
        kernel,
        out_shape=[jax.ShapeDtypeStruct((rows, points), jnp.bfloat16)] * EARLY,
        in_specs=[FAR] * 4,
        out_specs=[WHOLE] * EARLY,
        scratch_shapes=[
            pltpu.VMEM(extrap.shape, extrap.dtype),
            pltpu.VMEM(sources.shape, sources.dtype),
            pltpu.VMEM((EARLY * part,) + records.shape[1:], records.dtype),
            pltpu.VMEM(shots.shape, shots.dtype),
            pltpu.VMEM((EARLY * rows, points), jnp.bfloat16),
            pltpu.SemaphoreType.DMA((3 + SLICES,)),
        ],
        compiler_params=pltpu.CompilerParams(vmem_limit_bytes=56 << 20),
    )(extrap, sources, records, shots)


def rest(extrap, sources, records, shots, chunk_count):
    shot_count, _, points = sources.shape
    part = shot_count // chunk_count
    rows = 4 * part

    def kernel(extrap_ref, source_ref, record_ref, shot_ref, finished_ref, chunk_ref):
        @pl.when(lax.axis_index("depth") == 0)
        def _():
            fill(chunk_ref, shot_ref, source_ref, record_ref, EARLY, part)
            others = [finished_ref.at[chunk] for chunk in range(EARLY, chunk_count)]
            march(chunk_ref[...], extrap_ref, others)

    return pl.pallas_call(
        kernel,
        out_shape=jax.ShapeDtypeStruct((chunk_count, rows, points), jnp.bfloat16),
        in_specs=[WHOLE] * 4,
        out_specs=WHOLE,
        scratch_shapes=[pltpu.VMEM(((chunk_count - EARLY) * rows, points), jnp.bfloat16)],
        compiler_params=pltpu.CompilerParams(vmem_limit_bytes=16 << 20),
        cost_estimate=BRIEF,
    )(extrap, sources, records, shots)


def outer(source, record):
    return lax.dot_general(
        source, record, (((0,), (0,)), ((), ())), preferred_element_type=jnp.float32
    )


def correlate_own(finished, scale, part):
    chunk_count, _, points = finished.shape
    width = points // 2
    depth = 2 * chunk_count * part

    def kernel(finished_ref, scale_ref, out_ref, source_ref, record_ref):
        span = lax.axis_size("freq") // 2
        upper = (lax.axis_index("freq") // span) % 2
        column = pl.ds(pl.multiple_of(upper * width, width), width)
        for chunk in range(chunk_count):
            for index, (first, second) in enumerate(((0, 3), (2, 1))):
                row = pl.ds((2 * chunk + index) * part, part)
                source_ref[row] = finished_ref[chunk, pl.ds(first * part, part), column]
                record_ref[row] = finished_ref[chunk, pl.ds(second * part, part), :]
        out_ref[...] = outer(source_ref[...], record_ref[...]) * scale_ref[...]

    return pl.pallas_call(
        kernel,
        out_shape=jax.ShapeDtypeStruct((width, points), jnp.float32),
        in_specs=[WHOLE] * 2,
        out_specs=WHOLE,
        scratch_shapes=[
            pltpu.VMEM((depth, width), jnp.bfloat16),
            pltpu.VMEM((depth, points), jnp.bfloat16),
        ],
        compiler_params=pltpu.CompilerParams(vmem_limit_bytes=12 << 20),
        cost_estimate=BRIEF,
    )(finished, scale)


def correlate(own, theirs, unit, part):
    width, points = own.shape
    depth = 2 * sum(GROUPS) * part

    def kernel(own_ref, *refs):
        their_refs = refs[: len(theirs)]
        out_ref, source_ref, record_ref = refs[len(theirs) :]
        start = 0
        for group, ref in zip(GROUPS, their_refs):
            count = 2 * group * part
            source_ref[start : start + count] = ref[:count, points:]
            record_ref[start : start + count] = ref[:count, :points]
            start += count
        count = 2 * GROUPS[0] * part
        number = their_refs[0][count : count + 16, :128].astype(jnp.float32)[:1, :1]
        total = own_ref[...] + outer(source_ref[...], record_ref[...]) * (number * unit)
        out_ref[...] = total.astype(out_ref.dtype)

    return pl.pallas_call(
        kernel,
        out_shape=jax.ShapeDtypeStruct((width, points), jnp.bfloat16),
        in_specs=[WHOLE] * (1 + len(theirs)),
        out_specs=WHOLE,
        scratch_shapes=[
            pltpu.VMEM((depth, width), jnp.bfloat16),
            pltpu.VMEM((depth, points), jnp.bfloat16),
        ],
        compiler_params=pltpu.CompilerParams(vmem_limit_bytes=12 << 20),
    )(own, *theirs)


def angles(panel, angle_lag, depth_count):
    angle_count = angle_lag.shape[1]
    row_count = panel.shape[0] // depth_count
    points = panel.shape[1]

    def kernel(panel_ref, lag_ref, out_ref):
        total = None
        for lag in range(depth_count):
            column = (lag_ref[...] == lag).astype(jnp.bfloat16)
            skip = lag * row_count
            if row_count % 16 == 0:
                term = jnp.dot(panel_ref[skip:], column, preferred_element_type=jnp.float32)
            else:
                term = jnp.dot(panel_ref[...], column, preferred_element_type=jnp.float32)[skip:]
            if total is None:
                total = term
            elif skip:
                kept = total.shape[0] - skip
                total = jnp.concatenate([total[:kept] + term, total[kept:]], axis=0)
        total = total * (1.0 / math.sqrt(points))
        for depth in range(depth_count):
            out_ref[:, depth, :] = total[depth * row_count : (depth + 1) * row_count]

    return pl.pallas_call(
        kernel,
        out_shape=jax.ShapeDtypeStruct((row_count, depth_count, angle_count), jnp.float32),
        in_specs=[WHOLE] * 2,
        out_specs=WHOLE,
        compiler_params=pltpu.CompilerParams(vmem_limit_bytes=24 << 20),
    )(panel, angle_lag)


def shards(extrap, source_field, record_field, shot_of_record, freq_index, angle_lag):
    depth_count = lax.axis_size("depth")
    freq_count = lax.axis_size("freq")
    freq_slot = lax.axis_index("freq")
    points = source_field.shape[3]
    shot_count = source_field.shape[1]
    chunk_count = CHUNKS
    part = shot_count // chunk_count

    operator = extrap[0, 0]
    sources, records = source_field[0], record_field[0]
    firsts = head(operator, sources, records, shot_of_record, part)

    number = freq_index[0].astype(jnp.float32).reshape(1, 1) + 1.0
    span = freq_count // 2
    partner = [(slot, slot ^ span) for slot in range(freq_count)]

    sent = {}
    theirs = []
    round_count = first_round(depth_count - 1) + chunk_count
    for round_index in range(round_count):
        if round_index == EARLY:
            shots, _ = lax.optimization_barrier((shot_of_record, firsts[0]))
            finished = rest(operator, sources, records, shots, chunk_count)
        for parity in (0, 1):
            if not any(
                handled(round_index, level, chunk_count)
                for level in range(parity, depth_count, 2)
            ):
                continue
            pairs = [
                (level, level + 1)
                for level in senders(round_index, parity, depth_count, chunk_count)
            ]
            if round_index < EARLY:
                order = firsts[round_index]
            else:
                arrived = sent.get((1 - parity, round_index - LAGS[parity]), firsts[0])
                first = ()
                if parity == 0 and round_index < 2 * EARLY:
                    first = (firsts[round_index - EARLY],)
                *order, finished = extend(
                    arrived, operator, finished, round_index, parity, bool(pairs), first
                )
                order = order[0] if pairs else None
            if pairs:
                sent[parity, round_index] = lax.ppermute(order, "depth", pairs)
        stop = sum(GROUPS[: len(theirs) + 1])
        if len(theirs) < len(GROUPS) and round_index - first_round(depth_count - 1) == stop - 1:
            start = stop - GROUPS[len(theirs)]
            payload = pack(finished, number, start, stop, start == 0)
            payload, finished = lax.optimization_barrier((payload, finished))
            theirs.append(lax.ppermute(payload, "freq", partner))

    scale = 1.0 / (8 * freq_count) / math.sqrt(shot_count * freq_count)
    own = correlate_own(finished, number * scale, part)
    image = correlate(own, theirs, scale, part)
    width = points // 2
    span //= 2
    while span:
        width //= 2
        upper = (freq_slot // span) % 2 == 1
        partner = [(slot, slot ^ span) for slot in range(freq_count)]
        keep = jnp.where(upper, image[width:], image[:width])
        away = jnp.where(upper, image[:width], image[width:])
        received = lax.ppermute(away, "freq", partner)
        image = (keep.astype(jnp.float32) + received.astype(jnp.float32)).astype(jnp.bfloat16)
        span //= 2
    panel = lax.all_to_all(image, "depth", split_axis=0, concat_axis=0, tiled=True)
    return angles(panel, angle_lag, depth_count)


def solution(mesh):
    placed = (
        P("depth", "freq", None, None, None),
        P("freq", None, None, None),
        P("freq", None, None, None),
        P(),
        P("freq"),
        P(),
    )
    return jax.shard_map(
        shards,
        mesh=mesh,
        in_specs=placed,
        out_specs=P(("freq", "depth"), None, None),
        check_vma=False,
    )
```

```python
import math

import jax
import jax.numpy as jnp
from jax import lax
from jax.experimental import pallas as pl
from jax.experimental.pallas import tpu as pltpu
from jax.sharding import PartitionSpec as P

CHUNKS = 8
GROUPS = (3, 2, 2, 1)
LAGS = (3, 2)
EARLY = LAGS[1]
SLICES = 2

WHOLE = pl.BlockSpec(memory_space=pltpu.VMEM)
FAR = pl.BlockSpec(memory_space=pltpu.HBM)
BRIEF = pl.CostEstimate(flops=0, bytes_accessed=0, transcendentals=0)


def first_round(level):
    return sum(LAGS) * (level // 2) + LAGS[1] * (level % 2)


def handled(round_index, level, chunk_count):
    return 0 <= round_index - first_round(level) < chunk_count


def senders(round_index, parity, depth_count, chunk_count):
    everyone = list(range(parity, depth_count - 1, 2))
    levels = [level for level in everyone if handled(round_index, level, chunk_count)]
    if not levels or levels[0] == parity:
        return levels
    wanted = min(len(everyone), -(-chunk_count // sum(LAGS)))
    first, last = everyone.index(levels[0]), everyone.index(levels[-1])
    return everyone[first : max(first + wanted, last + 1)]


def march(values, extrap_ref, out_refs):
    real = jnp.dot(values, extrap_ref[0], preferred_element_type=jnp.float32)
    imag = jnp.dot(values, extrap_ref[1], preferred_element_type=jnp.float32)
    combine(real, imag, out_refs)


def combine(real, imag, out_refs):
    rows = out_refs[0].shape[0]
    half = rows // 2
    for chunk, out_ref in enumerate(out_refs):
        upper = slice(chunk * rows, chunk * rows + half)
        lower = slice(chunk * rows + half, (chunk + 1) * rows)
        out_ref[:half] = (real[upper] - imag[lower]).astype(out_ref.dtype)
        out_ref[half:] = (imag[upper] + real[lower]).astype(out_ref.dtype)


def extend(arrived, extrap, finished, round_index, parity, sends, first=()):
    rows, points = arrived.shape
    chunk_count = finished.shape[0]

    def kernel(arrived_ref, extrap_ref, finished_in, *refs):
        finished_ref = refs[-1]
        level = lax.axis_index("depth")
        chunk = round_index - first_round(level)
        mine = (level > 0) & (level % 2 == parity) & (chunk >= 0) & (chunk < chunk_count)
        place_ref = finished_ref.at[jnp.clip(chunk, 0, chunk_count - 1)]
        out_ref = refs[-2] if sends else place_ref

        @pl.when(mine)
        def _():
            march(arrived_ref[...], extrap_ref, [out_ref])

        if sends:

            @pl.when(mine)
            def _():
                place_ref[...] = out_ref[...]

            if parity == 0 and round_index < chunk_count:

                @pl.when(level == 0)
                def _():
                    out_ref[...] = finished_ref[round_index]
                    if first:
                        finished_ref[round_index - EARLY] = refs[0][...]

    kept = jax.ShapeDtypeStruct(finished.shape, finished.dtype)
    sent = jax.ShapeDtypeStruct((rows, points), jnp.bfloat16)
    return pl.pallas_call(
        kernel,
        out_shape=[sent, kept] if sends else [kept],
        in_specs=[WHOLE] * (3 + len(first)),
        out_specs=[WHOLE, WHOLE] if sends else [WHOLE],
        input_output_aliases={2: 1 if sends else 0},
        compiler_params=pltpu.CompilerParams(vmem_limit_bytes=8 << 20),
        cost_estimate=BRIEF,
    )(arrived, extrap, finished, *first)


def pack(finished, number, start, stop, noted):
    rows, points = finished.shape[1:]
    part = rows // 4
    half = points // 2
    count = 2 * part * (stop - start)

    def kernel(finished_ref, number_ref, out_ref):
        span = lax.axis_size("freq") // 2
        upper = (lax.axis_index("freq") // span) % 2
        column = pl.ds(pl.multiple_of((1 - upper) * half, half), half)
        for chunk in range(start, stop):
            for index, (first, second) in enumerate(((0, 3), (2, 1))):
                row = pl.ds((2 * (chunk - start) + index) * part, part)
                out_ref[row, :points] = finished_ref[chunk, pl.ds(second * part, part), :]
                out_ref[row, points:] = finished_ref[chunk, pl.ds(first * part, part), column]
        if noted:
            out_ref[count:] = jnp.broadcast_to(
                number_ref[...].astype(out_ref.dtype), (16, out_ref.shape[1])
            )

    return pl.pallas_call(
        kernel,
        out_shape=jax.ShapeDtypeStruct((count + 16 * noted, points + half), jnp.bfloat16),
        in_specs=[WHOLE] * 2,
        out_specs=WHOLE,
        compiler_params=pltpu.CompilerParams(vmem_limit_bytes=8 << 20),
        cost_estimate=BRIEF,
    )(finished, number)


def fill(out_ref, shot_ref, source_ref, record_ref, first, part):
    shot_count = source_ref.shape[0]
    chunk_count = out_ref.shape[0] // (4 * part)
    count = shot_count if first else chunk_count * part
    pick = (
        shot_ref[:count][None, :] == lax.broadcasted_iota(jnp.int32, (shot_count, count), 0)
    ).astype(jnp.bfloat16)

    def picked(component):
        return lax.dot_general(
            pick,
            source_ref[:, component, :],
            (((0,), (0,)), ((), ())),
            preferred_element_type=jnp.float32,
        ).astype(jnp.bfloat16)

    for place, values in (
        (0, picked(0)),
        (1, record_ref[:, 1, :]),
        (2, picked(1)),
        (3, record_ref[:, 0, :]),
    ):
        for chunk in range(chunk_count):
            row = (4 * chunk + place) * part
            shot = (first + chunk) * part
            out_ref[row : row + part] = values[shot : shot + part]


def head(extrap, sources, records, shots, part):
    points = extrap.shape[2]
    rows = 4 * part

    def kernel(extrap_hbm, source_hbm, record_hbm, shot_hbm, *refs):
        out_refs = refs[:EARLY]
        extrap_ref, source_ref, record_ref, shot_ref, chunk_ref, sems = refs[EARLY:]

        @pl.when(lax.axis_index("depth") == 0)
        def _():
            copies = [
                pltpu.make_async_copy(shot_hbm, shot_ref, sems.at[0]),
                pltpu.make_async_copy(source_hbm, source_ref, sems.at[1]),
                pltpu.make_async_copy(record_hbm.at[pl.ds(0, EARLY * part)], record_ref, sems.at[2]),
            ]
            bands = [pl.ds(index * points // SLICES, points // SLICES) for index in range(SLICES)]
            copies += [
                pltpu.make_async_copy(
                    extrap_hbm.at[:, band], extrap_ref.at[:, band], sems.at[3 + index]
                )
                for index, band in enumerate(bands)
            ]
            for copy in copies:
                copy.start()
            for copy in copies[:3]:
                copy.wait()
            fill(chunk_ref, shot_ref, source_ref, record_ref, 0, part)
            real = imag = 0.0
            for copy, band in zip(copies[3:], bands):
                copy.wait()
                values = chunk_ref[:, band]
                real += jnp.dot(values, extrap_ref[0, band], preferred_element_type=jnp.float32)
                imag += jnp.dot(values, extrap_ref[1, band], preferred_element_type=jnp.float32)
            combine(real, imag, out_refs)

    return pl.pallas_call(
        kernel,
        out_shape=[jax.ShapeDtypeStruct((rows, points), jnp.bfloat16)] * EARLY,
        in_specs=[FAR] * 4,
        out_specs=[WHOLE] * EARLY,
        scratch_shapes=[
            pltpu.VMEM(extrap.shape, extrap.dtype),
            pltpu.VMEM(sources.shape, sources.dtype),
            pltpu.VMEM((EARLY * part,) + records.shape[1:], records.dtype),
            pltpu.VMEM(shots.shape, shots.dtype),
            pltpu.VMEM((EARLY * rows, points), jnp.bfloat16),
            pltpu.SemaphoreType.DMA((3 + SLICES,)),
        ],
        compiler_params=pltpu.CompilerParams(vmem_limit_bytes=56 << 20),
    )(extrap, sources, records, shots)


def rest(extrap, sources, records, shots, chunk_count):
    shot_count, _, points = sources.shape
    part = shot_count // chunk_count
    rows = 4 * part

    def kernel(extrap_ref, source_ref, record_ref, shot_ref, finished_ref, chunk_ref):
        @pl.when(lax.axis_index("depth") == 0)
        def _():
            fill(chunk_ref, shot_ref, source_ref, record_ref, EARLY, part)
            others = [finished_ref.at[chunk] for chunk in range(EARLY, chunk_count)]
            march(chunk_ref[...], extrap_ref, others)

    return pl.pallas_call(
        kernel,
        out_shape=jax.ShapeDtypeStruct((chunk_count, rows, points), jnp.bfloat16),
        in_specs=[WHOLE] * 4,
        out_specs=WHOLE,
        scratch_shapes=[pltpu.VMEM(((chunk_count - EARLY) * rows, points), jnp.bfloat16)],
        compiler_params=pltpu.CompilerParams(vmem_limit_bytes=16 << 20),
        cost_estimate=BRIEF,
    )(extrap, sources, records, shots)


def outer(source, record):
    return lax.dot_general(
        source, record, (((0,), (0,)), ((), ())), preferred_element_type=jnp.float32
    )


def correlate_own(finished, scale, part):
    chunk_count, _, points = finished.shape
    width = points // 2
    depth = 2 * chunk_count * part

    def kernel(finished_ref, scale_ref, out_ref, source_ref, record_ref):
        span = lax.axis_size("freq") // 2
        upper = (lax.axis_index("freq") // span) % 2
        column = pl.ds(pl.multiple_of(upper * width, width), width)
        for chunk in range(chunk_count):
            for index, (first, second) in enumerate(((0, 3), (2, 1))):
                row = pl.ds((2 * chunk + index) * part, part)
                source_ref[row] = finished_ref[chunk, pl.ds(first * part, part), column]
                record_ref[row] = finished_ref[chunk, pl.ds(second * part, part), :]
        out_ref[...] = outer(source_ref[...], record_ref[...]) * scale_ref[...]

    return pl.pallas_call(
        kernel,
        out_shape=jax.ShapeDtypeStruct((width, points), jnp.float32),
        in_specs=[WHOLE] * 2,
        out_specs=WHOLE,
        scratch_shapes=[
            pltpu.VMEM((depth, width), jnp.bfloat16),
            pltpu.VMEM((depth, points), jnp.bfloat16),
        ],
        compiler_params=pltpu.CompilerParams(vmem_limit_bytes=12 << 20),
        cost_estimate=BRIEF,
    )(finished, scale)


def correlate(own, theirs, unit, part, away):
    width, points = own.shape
    width //= 2
    depth = 2 * sum(GROUPS) * part

    def kernel(own_ref, *refs):
        their_refs = refs[: len(theirs)]
        out_ref, source_ref, record_ref = refs[len(theirs) :]
        upper = (lax.axis_index("freq") // (lax.axis_size("freq") // 4)) % 2
        place = pl.multiple_of((1 - upper if away else upper) * width, width)
        column = pl.ds(pl.multiple_of(points + place, width), width)
        start = 0
        for group, ref in zip(GROUPS, their_refs):
            count = 2 * group * part
            source_ref[start : start + count] = ref[pl.ds(0, count), column]
            record_ref[start : start + count] = ref[:count, :points]
            start += count
        count = 2 * GROUPS[0] * part
        number = their_refs[0][count : count + 16, :128].astype(jnp.float32)[:1, :1]
        total = own_ref[pl.ds(place, width)] + outer(source_ref[...], record_ref[...]) * (number * unit)
        out_ref[...] = total.astype(out_ref.dtype)

    return pl.pallas_call(
        kernel,
        out_shape=jax.ShapeDtypeStruct((width, points), jnp.bfloat16),
        in_specs=[WHOLE] * (1 + len(theirs)),
        out_specs=WHOLE,
        scratch_shapes=[
            pltpu.VMEM((depth, width), jnp.bfloat16),
            pltpu.VMEM((depth, points), jnp.bfloat16),
        ],
        compiler_params=pltpu.CompilerParams(vmem_limit_bytes=12 << 20),
    )(own, *theirs)


def angles(panel, angle_lag, depth_count):
    angle_count = angle_lag.shape[1]
    row_count = panel.shape[0] // depth_count
    points = panel.shape[1]

    def kernel(panel_ref, lag_ref, out_ref):
        total = None
        for lag in range(depth_count):
            column = (lag_ref[...] == lag).astype(jnp.bfloat16)
            skip = lag * row_count
            if row_count % 16 == 0:
                term = jnp.dot(panel_ref[skip:], column, preferred_element_type=jnp.float32)
            else:
                term = jnp.dot(panel_ref[...], column, preferred_element_type=jnp.float32)[skip:]
            if total is None:
                total = term
            elif skip:
                kept = total.shape[0] - skip
                total = jnp.concatenate([total[:kept] + term, total[kept:]], axis=0)
        total = total * (1.0 / math.sqrt(points))
        for depth in range(depth_count):
            out_ref[:, depth, :] = total[depth * row_count : (depth + 1) * row_count]

    return pl.pallas_call(
        kernel,
        out_shape=jax.ShapeDtypeStruct((row_count, depth_count, angle_count), jnp.float32),
        in_specs=[WHOLE] * 2,
        out_specs=WHOLE,
        compiler_params=pltpu.CompilerParams(vmem_limit_bytes=24 << 20),
    )(panel, angle_lag)


def shards(extrap, source_field, record_field, shot_of_record, freq_index, angle_lag):
    depth_count = lax.axis_size("depth")
    freq_count = lax.axis_size("freq")
    freq_slot = lax.axis_index("freq")
    points = source_field.shape[3]
    shot_count = source_field.shape[1]
    chunk_count = CHUNKS
    part = shot_count // chunk_count

    operator = extrap[0, 0]
    sources, records = source_field[0], record_field[0]
    firsts = head(operator, sources, records, shot_of_record, part)

    number = freq_index[0].astype(jnp.float32).reshape(1, 1) + 1.0
    span = freq_count // 2
    partner = [(slot, slot ^ span) for slot in range(freq_count)]

    sent = {}
    theirs = []
    round_count = first_round(depth_count - 1) + chunk_count
    for round_index in range(round_count):
        if round_index == EARLY:
            shots, _ = lax.optimization_barrier((shot_of_record, firsts[0]))
            finished = rest(operator, sources, records, shots, chunk_count)
        for parity in (0, 1):
            if not any(
                handled(round_index, level, chunk_count)
                for level in range(parity, depth_count, 2)
            ):
                continue
            pairs = [
                (level, level + 1)
                for level in senders(round_index, parity, depth_count, chunk_count)
            ]
            if round_index < EARLY:
                order = firsts[round_index]
            else:
                arrived = sent.get((1 - parity, round_index - LAGS[parity]), firsts[0])
                first = ()
                if parity == 0 and round_index < 2 * EARLY:
                    first = (firsts[round_index - EARLY],)
                *order, finished = extend(
                    arrived, operator, finished, round_index, parity, bool(pairs), first
                )
                order = order[0] if pairs else None
            if pairs:
                sent[parity, round_index] = lax.ppermute(order, "depth", pairs)
        stop = sum(GROUPS[: len(theirs) + 1])
        if len(theirs) < len(GROUPS) and round_index - first_round(depth_count - 1) == stop - 1:
            start = stop - GROUPS[len(theirs)]
            payload = pack(finished, number, start, stop, start == 0)
            payload, finished = lax.optimization_barrier((payload, finished))
            theirs.append(lax.ppermute(payload, "freq", partner))

    scale = 1.0 / (8 * freq_count) / math.sqrt(shot_count * freq_count)
    own = correlate_own(finished, number * scale, part)
    away, keep = (correlate(own, theirs, scale, part, side) for side in (True, False))
    width = points // 4
    span //= 2
    partner = [(slot, slot ^ span) for slot in range(freq_count)]
    received = lax.ppermute(away, "freq", partner)
    image = (keep.astype(jnp.float32) + received.astype(jnp.float32)).astype(jnp.bfloat16)
    span //= 2
    while span:
        width //= 2
        upper = (freq_slot // span) % 2 == 1
        partner = [(slot, slot ^ span) for slot in range(freq_count)]
        keep = jnp.where(upper, image[width:], image[:width])
        away = jnp.where(upper, image[:width], image[width:])
        received = lax.ppermute(away, "freq", partner)
        image = (keep.astype(jnp.float32) + received.astype(jnp.float32)).astype(jnp.bfloat16)
        span //= 2
    panel = lax.all_to_all(image, "depth", split_axis=0, concat_axis=0, tiled=True)
    return angles(panel, angle_lag, depth_count)


def solution(mesh):
    placed = (
        P("depth", "freq", None, None, None),
        P("freq", None, None, None),
        P("freq", None, None, None),
        P(),
        P("freq"),
        P(),
    )
    return jax.shard_map(
        shards,
        mesh=mesh,
        in_specs=placed,
        out_specs=P(("freq", "depth"), None, None),
        check_vma=False,
    )
```
